32 devices in a mesh: obj: 4 (over y, core), scan: 8 (over z, x).
Axes of the slice: x: 2, y: 2, z: 4, core: 2. Of those that a mesh axis runs over, the one named last changes fastest.
Arguments:
- object_slab: float32 [2, 2, 1536, 4096], P(None, None, 'obj', 'scan'), may hold values from -4 to 4
- probe_mode_stack: float32 [6, 2, 256, 256], replicated, may hold values from -2 to 2
- offsets: int32 [96, 2], P(('obj', 'scan')), may hold values from 0 to 3840, as said below
- measured: float32 [96, 256, 256], P(('obj', 'scan')), may hold values from 0.05 to 3
- counts: int32 [32], P(('obj', 'scan')), may hold values from 1 to 3, as said below
Outputs:
- new_object: float32 [2, 2, 1536, 4096], P(None, None, 'obj', 'scan')
- new_probe: float32 [6, 2, 256, 256], replicated
The draws below stay inside these ranges and needn't reach their ends.
Inputs may be any that keep to these rules, and one draw needn't show every extreme that they name: `offsets`: rows 3 d to 3 d + 2 belong to device d (devices in the order obj, then scan). Each row gives the object row and column of a patch's top-left pixel; that pixel lies in the device's own tile of 384 x 512 pixels, and the whole 256 x 256 patch lies inside the object. Device d uses its first counts[d] position slots; the others are ignored.
All inputs are finite; a program needn't handle non-finite values.
Results may differ from the reference program's by a relative error of at most 0.008.
The reference program's roundings to bfloat16 on the way count: a program that leaves them out, or rounds other values in their place, can miss the bound.
Values sent between devices are 32-bit elements; how exact they have to be, the bound alone decides.
A program may use at most 128 MiB of HBM per device.

```python
import math
import jax
import jax.numpy as jnp
from jax import lax

P_SIZE = 256
M = 6
SL = 2
TH = 384
TW = 512
CAP = 3
OH = 1536
OW = 4096
POSITIONS = 96
DEVICES = 32


def draw_offsets(key, part):
    row_ids = jnp.arange(CAP * DEVICES, dtype=jnp.int32)
    device = row_ids // CAP
    tiles_across = OW // TW
    tile_row = device // tiles_across
    tile_col = device % tiles_across
    lowest_row = tile_row * TH
    highest_row = jnp.minimum(lowest_row + TH, OH - P_SIZE + 1)
    lowest_col = tile_col * TW
    highest_col = jnp.minimum(lowest_col + TW, OW - P_SIZE + 1)
    key_rows, key_cols = jax.random.split(key)
    row_value = jax.random.randint(key_rows, row_ids.shape, lowest_row, highest_row)
    col_value = jax.random.randint(key_cols, row_ids.shape, lowest_col, highest_col)
    last_slot = CAP * (DEVICES - 1)
    row_value = row_value.at[0].set(0).at[last_slot].set(OH - P_SIZE)
    col_value = col_value.at[0].set(0).at[last_slot].set(OW - P_SIZE)
    return jnp.stack([row_value, col_value], axis=1).astype(jnp.int32)


def draw_counts(key, part):
    key_ticket, key_chosen = jax.random.split(key)
    ticket = jax.random.randint(key_ticket, (DEVICES,), 0, 20)
    used_slots = jnp.where(ticket < 12, 1, jnp.where(ticket < 15, 2, CAP))
    used_slots = jnp.minimum(used_slots, CAP)
    chosen = jax.random.randint(key_chosen, (), 0, DEVICES)
    used_slots = used_slots.at[chosen].set(CAP)
    return used_slots.astype(jnp.int32)


def level_of(key, shape, cuts, smallest, top_value):
    def one(axis_at, shards_of):
        steps = jax.random.uniform(jax.random.fold_in(jax.random.fold_in(key, 6), axis_at), (shards_of,), jnp.float32, smallest / len(cuts), top_value / len(cuts))
        return jnp.repeat(jnp.exp(steps), shape[axis_at] // shards_of).reshape((-1,) + (1,) * (len(shape) - axis_at - 1))

    level = one(*cuts[0])
    for cut in cuts[1:]:
        level = level * one(*cut)
    return level


def bell_draw(stream_key, dims, scale, most, cuts=(), kind=jnp.bfloat16):
    level = level_of(stream_key, dims, cuts, -0.22, 0.18) if cuts else 1.0
    array = jax.random.normal(stream_key, dims, jnp.float32) * scale * level
    return jnp.minimum(jnp.maximum(array, -most), most).astype(kind)


def setup_inputs(seed: int = 0) -> dict:
    seeds = jax.random.split(jax.random.key(seed), 6)
    return {
        "object_slab": bell_draw(seeds[0], (SL, 2, OH, OW), 0.7, 4.0, ((2, 4), (3, 8)), jnp.float32),
        "probe_mode_stack": bell_draw(seeds[1], (M, 2, P_SIZE, P_SIZE), 0.3, 2.0, (), jnp.float32),
        "offsets": draw_offsets(jax.random.fold_in(seeds[5], 71), 0),
        "measured": jnp.clip(jnp.exp(math.log(3.0) - 4.0943445 * jax.random.uniform(seeds[3], (POSITIONS, P_SIZE, P_SIZE), jnp.float32) ** level_of(seeds[3], (POSITIONS, P_SIZE, P_SIZE), ((0, 32),), -0.2, 0.2)), 0.05, 3.0),
        "counts": draw_counts(jax.random.fold_in(seeds[5], 71), 0),
    }


chirp_scale = 24.0
probe_step = 0.15

def dft_table(pattern, sign_factor):
    indices = jnp.arange(pattern, dtype=jnp.int32)
    phases = indices[:, None] * indices[None, :] % pattern
    angles = phases.astype(jnp.float32) * (2.0 * math.pi / pattern)
    normalizer = 1.0 / math.sqrt(pattern)
    real_part = jnp.cos(angles) * normalizer
    imag_part = sign_factor * jnp.sin(angles) * normalizer
    row_real = jnp.stack([real_part, -imag_part], axis=1)
    row_imag = jnp.stack([imag_part, real_part], axis=1)
    return jnp.stack([row_real, row_imag], axis=0).astype(jnp.bfloat16)

def propagator(pattern):
    indices = jnp.arange(pattern, dtype=jnp.int32)
    freqs = ((indices + pattern // 2) % pattern - pattern // 2).astype(jnp.float32) / pattern
    phases = -math.pi * chirp_scale * (freqs[:, None] ** 2 + freqs[None, :] ** 2)
    return jnp.stack([jnp.cos(phases), jnp.sin(phases)], axis=0)

def transform(field_in, tables):
    half_done = jnp.einsum('dkcy,mcyx->mdkx', tables.astype(jnp.float32), field_in.astype(jnp.float32))
    half_done = half_done.astype(jnp.bfloat16)
    return jnp.einsum('mcyx,dkcx->mdyk', half_done.astype(jnp.float32), tables.astype(jnp.float32))

def complex_times(left_arr, right_arr):
    left_real, left_imag = (left_arr[..., 0, :, :], left_arr[..., 1, :, :])
    right_real, right_imag = (right_arr[..., 0, :, :], right_arr[..., 1, :, :])
    return jnp.stack([left_real * right_real - left_imag * right_imag, left_real * right_imag + left_imag * right_real], axis=-3)

def conjugate(values):
    return jnp.stack([values[..., 0, :, :], -values[..., 1, :, :]], axis=-3)

def position_updates(object_window, probe_mode_stack, measured_pattern, propagate_forward, propagate_backward, fresnel_kernel):
    layers = object_window.shape[0]
    wavefield = probe_mode_stack
    inputs = []
    exit_wave = wavefield
    for layer_index in range(layers):
        inputs.append(wavefield)
        exit_wave = complex_times(object_window[layer_index], wavefield)
        if layer_index < layers - 1:
            spectrum = transform(exit_wave.astype(jnp.bfloat16), propagate_forward)
            wavefield = transform(complex_times(fresnel_kernel, spectrum).astype(jnp.bfloat16), propagate_backward)
    detector_wavefront = transform(exit_wave.astype(jnp.bfloat16), propagate_forward)
    modal_intensity = lax.optimization_barrier(jnp.sum(detector_wavefront[:, 0] ** 2 + detector_wavefront[:, 1] ** 2, axis=0))
    amplitude_residual = ((modal_intensity - measured_pattern)[None, None] * detector_wavefront).astype(jnp.bfloat16)
    gradient = transform(amplitude_residual, propagate_backward)
    pieces = [None] * layers
    for layer_index in reversed(range(layers)):
        if layer_index < layers - 1:
            spectrum = transform(gradient.astype(jnp.bfloat16), propagate_forward)
            gradient = transform(complex_times(conjugate(fresnel_kernel), spectrum).astype(jnp.bfloat16), propagate_backward)
        pieces[layer_index] = lax.optimization_barrier(jnp.sum(complex_times(conjugate(inputs[layer_index]), gradient), axis=0))
        gradient = complex_times(conjugate(object_window[layer_index]), gradient)
    return (jnp.stack(pieces, axis=0), gradient)

def reference(object_slab, probe_mode_stack, offsets, measured, counts):
    layers = object_slab.shape[0]
    propagate_forward = dft_table(P_SIZE, -1.0)
    propagate_backward = dft_table(P_SIZE, 1.0)
    fresnel_kernel = propagator(P_SIZE)
    lamp_power = lax.optimization_barrier(jnp.sum(probe_mode_stack[:, 0] ** 2 + probe_mode_stack[:, 1] ** 2, axis=0))
    row_ids = jnp.arange(POSITIONS, dtype=jnp.int32)
    is_used = row_ids % CAP < counts[row_ids // CAP]
    zero_index = jnp.int32(0)

    def visit_slot(state_now, current_entry):
        scan_offset, measured_pattern, visited_marker = current_entry

        def active(inner_state):
            grad_object, illumination, grad_probe = inner_state
            corner_at = (zero_index, zero_index, scan_offset[0].astype(jnp.int32), scan_offset[1].astype(jnp.int32))
            object_window = lax.dynamic_slice(object_slab, corner_at, (layers, 2, P_SIZE, P_SIZE))
            object_update, probe_update = position_updates(object_window, probe_mode_stack, measured_pattern, propagate_forward, propagate_backward, fresnel_kernel)
            previous = lax.dynamic_slice(grad_object, corner_at, (layers, 2, P_SIZE, P_SIZE))
            grad_object = lax.dynamic_update_slice(grad_object, previous + object_update, corner_at)
            light_at = (scan_offset[0].astype(jnp.int32), scan_offset[1].astype(jnp.int32))
            previous_light = lax.dynamic_slice(illumination, light_at, (P_SIZE, P_SIZE))
            illumination = lax.dynamic_update_slice(illumination, previous_light + lamp_power, light_at)
            return (grad_object, illumination, grad_probe + probe_update)
        return (lax.cond(visited_marker, active, lambda inner_state: inner_state, state_now), None)
    start_state = (jnp.zeros(object_slab.shape, jnp.float32), jnp.zeros(object_slab.shape[2:], jnp.float32), jnp.zeros(probe_mode_stack.shape, jnp.float32))
    final_state, _ = lax.scan(visit_slot, start_state, (offsets, measured, is_used))
    grad_object, illumination, grad_probe = final_state
    new_object = object_slab - grad_object / (illumination + 1.0)
    grad_scale = jnp.sqrt(jnp.mean(grad_probe * grad_probe) + 1e-06)
    new_probe = probe_mode_stack - probe_step * grad_probe / grad_scale
    return (new_object, new_probe)
```

```python
import functools
import math

import jax
import jax.numpy as jnp
import numpy as np
from jax import lax
from jax.experimental import pallas as pl
from jax.experimental.pallas import tpu as pltpu
from jax.sharding import PartitionSpec as P

chirp_scale = 24.0
probe_step = 0.15
lanes = 128
sublanes = 8
vmem_bytes = 56 * 1024 * 1024


def from_behind(array, axis, by):
    count = lax.axis_size(axis)
    pairs = [(i, i + by) for i in range(count) if 0 <= i + by < count]
    return lax.ppermute(array, axis, pairs)


def dft_matrix(pattern, sign_factor):
    indices = np.arange(pattern)
    angles = (indices[:, None] * indices[None, :] % pattern) * (2.0 * math.pi / pattern)
    real_part = np.cos(angles) / math.sqrt(pattern)
    imag_part = sign_factor * np.sin(angles) / math.sqrt(pattern)
    upper = np.concatenate([real_part, -imag_part], axis=1)
    lower = np.concatenate([imag_part, real_part], axis=1)
    return jnp.asarray(np.concatenate([upper, lower], axis=0).astype(np.float32), jnp.bfloat16)


def propagator(pattern):
    indices = np.arange(pattern)
    freqs = ((indices + pattern // 2) % pattern - pattern // 2) / pattern
    phases = -math.pi * chirp_scale * (freqs[:, None] ** 2 + freqs[None, :] ** 2)
    return jnp.asarray(np.stack([np.cos(phases), np.sin(phases)], axis=0).astype(np.float32))


def aligned(row, col):
    row_base = pl.multiple_of(row // sublanes * sublanes, sublanes)
    col_base = pl.multiple_of(col // lanes * lanes, lanes)
    return row_base, col_base, row - row_base, col - col_base


def pad(array):
    array = jnp.concatenate([array, jnp.zeros((array.shape[0], lanes), jnp.float32)], axis=1)
    return jnp.concatenate([array, jnp.zeros((sublanes, array.shape[1]), jnp.float32)], axis=0)


def roll_down(array, rows, cols):
    return pltpu.roll(pltpu.roll(array, cols, 1), rows, 0)


def transform(real_part, imag_part, left, right):
    pattern = real_part.shape[0]
    stacked = jnp.concatenate([real_part.astype(jnp.bfloat16), imag_part.astype(jnp.bfloat16)], axis=0)
    half = jnp.dot(left, stacked, preferred_element_type=jnp.float32).astype(jnp.bfloat16)
    half = jnp.concatenate([half[:pattern], half[pattern:]], axis=1)
    full = jnp.dot(half, right, preferred_element_type=jnp.float32)
    return full[:, :pattern], full[:, pattern:]


def slots_kernel(
    corners, used, tile, right, lower, corner, probe, measured, table_f, table_b, fresnel,
    grad_tile, grad_right, grad_lower, grad_corner, grad_probe,
    ext, grad, window, waves, far, intensity, term, sems_in, sems_out,
):
    modes, _, pattern, _ = probe.shape
    layers = tile.shape[0]
    height, width = tile.shape[2], tile.shape[3]
    wide = pattern + lanes
    tall = pattern + sublanes

    def spots(buffer):
        return (
            buffer.at[:, :, pl.ds(0, height), pl.ds(0, width)],
            buffer.at[:, :, pl.ds(0, height), pl.ds(width, pattern)],
            buffer.at[:, :, pl.ds(height, pattern), pl.ds(0, width)],
            buffer.at[:, :, pl.ds(height, pattern), pl.ds(width, pattern)],
        )

    loads = [
        pltpu.make_async_copy(source, spot, sems_in.at[k])
        for k, (source, spot) in enumerate(zip((tile, right, lower, corner), spots(ext)))
    ]
    for load in loads:
        load.start()
    grad[...] = jnp.zeros_like(grad)
    grad_probe[...] = jnp.zeros_like(grad_probe)
    for load in loads:
        load.wait()

    @pl.loop(0, used[0])
    def _(slot):
        row = corners[slot, 0]
        col = corners[slot, 1]
        row_base, col_base, row_shift, col_shift = aligned(row, col)
        row_back = jnp.where(row_shift == 0, 0, tall - row_shift)
        col_back = jnp.where(col_shift == 0, 0, wide - col_shift)
        for layer in range(layers):
            for part in range(2):
                block = ext[layer, part, pl.ds(row_base, tall), pl.ds(col_base, wide)]
                window[layer, part] = roll_down(block, row_back, col_back)[:pattern, :pattern]
        intensity[...] = jnp.zeros_like(intensity)
        term[...] = jnp.zeros_like(term)

        @pl.loop(0, modes)
        def _(mode):
            wr, wi = probe[mode, 0], probe[mode, 1]
            for layer in range(layers):
                o_r, o_i = window[layer, 0], window[layer, 1]
                fr, fi = transform(o_r * wr - o_i * wi, o_r * wi + o_i * wr, table_f[...], table_b[...])
                if layer < layers - 1:
                    hr, hi = fresnel[0], fresnel[1]
                    wr, wi = transform(hr * fr - hi * fi, hr * fi + hi * fr, table_b[...], table_f[...])
                    waves[layer, mode, 0] = wr
                    waves[layer, mode, 1] = wi
            far[mode, 0] = fr
            far[mode, 1] = fi
            intensity[...] += fr * fr + fi * fi

        intensity[...] = intensity[...] - measured[slot]

        @pl.loop(0, modes)
        def _(mode):
            gain = intensity[...]
            gr, gi = transform(gain * far[mode, 0], gain * far[mode, 1], table_b[...], table_f[...])
            for layer in reversed(range(layers)):
                if layer < layers - 1:
                    sr, si = transform(gr, gi, table_f[...], table_b[...])
                    hr, hi = fresnel[0], fresnel[1]
                    gr, gi = transform(hr * sr + hi * si, hr * si - hi * sr, table_b[...], table_f[...])
                if layer == 0:
                    wr, wi = probe[mode, 0], probe[mode, 1]
                else:
                    wr, wi = waves[layer - 1, mode, 0], waves[layer - 1, mode, 1]
                term[layer, 0] += wr * gr + wi * gi
                term[layer, 1] += wr * gi - wi * gr
                o_r, o_i = window[layer, 0], window[layer, 1]
                gr, gi = o_r * gr + o_i * gi, o_r * gi - o_i * gr
            grad_probe[mode, 0] += gr
            grad_probe[mode, 1] += gi

        for layer in range(layers):
            for part in range(2):
                at = (layer, part, pl.ds(row_base, tall), pl.ds(col_base, wide))
                grad[at] = grad[at] + roll_down(pad(term[layer, part]), row_shift, col_shift)

    saves = [
        pltpu.make_async_copy(spot, target, sems_out.at[k])
        for k, (spot, target) in enumerate(
            zip(spots(grad), (grad_tile, grad_right, grad_lower, grad_corner))
        )
    ]
    for save in saves:
        save.start()
    for save in saves:
        save.wait()


def run_slots(corners, used, tile, right, lower, corner, probe, measured, table_f, table_b, fresnel):
    layers, _, height, width = tile.shape
    modes, _, pattern, _ = probe.shape
    smem = pl.BlockSpec(memory_space=pltpu.SMEM)
    vmem = pl.BlockSpec(memory_space=pltpu.VMEM)
    anyw = pl.BlockSpec(memory_space=pl.ANY)
    f32 = jnp.float32
    ext_shape = (layers, 2, height + pattern, width + pattern)
    return pl.pallas_call(
        slots_kernel,
        out_shape=(
            jax.ShapeDtypeStruct(tile.shape, f32),
            jax.ShapeDtypeStruct(right.shape, f32),
            jax.ShapeDtypeStruct(lower.shape, f32),
            jax.ShapeDtypeStruct(corner.shape, f32),
            jax.ShapeDtypeStruct(probe.shape, f32),
        ),
        in_specs=[smem, smem, anyw, anyw, anyw, anyw, vmem, vmem, vmem, vmem, vmem],
        out_specs=(anyw, anyw, anyw, anyw, vmem),
        scratch_shapes=[
            pltpu.VMEM(ext_shape, f32),
            pltpu.VMEM(ext_shape, f32),
            pltpu.VMEM((layers, 2, pattern, pattern), f32),
            pltpu.VMEM((layers - 1, modes, 2, pattern, pattern), f32),
            pltpu.VMEM((modes, 2, pattern, pattern), f32),
            pltpu.VMEM((pattern, pattern), f32),
            pltpu.VMEM((layers, 2, pattern, pattern), f32),
            pltpu.SemaphoreType.DMA((4,)),
            pltpu.SemaphoreType.DMA((4,)),
        ],
        compiler_params=pltpu.CompilerParams(vmem_limit_bytes=vmem_bytes),
        cost_estimate=pl.CostEstimate(flops=29_000_000_000, bytes_accessed=30_000_000, transcendentals=0),
    )(corners, used, tile, right, lower, corner, probe, measured, table_f, table_b, fresnel)


def light_kernel(height, width, slots, info, probe, light, canvas, power):
    modes, _, pattern, _ = probe.shape
    total = jnp.zeros((pattern, pattern), jnp.float32)
    for mode in range(modes):
        total = total + (probe[mode, 0] * probe[mode, 0] + probe[mode, 1] * probe[mode, 1])
    power[...] = pad(total)
    canvas[...] = jnp.zeros_like(canvas)
    for block in range(4):
        base = block * (2 * slots + 1)

        @pl.loop(0, info[base + 2 * slots])
        def _(slot):
            row = info[base + 2 * slot] + height
            col = info[base + 2 * slot + 1] + width
            row_base, col_base, row_shift, col_shift = aligned(row, col)
            at = (pl.ds(row_base, pattern + sublanes), pl.ds(col_base, pattern + lanes))
            canvas[at] = canvas[at] + roll_down(power[...], row_shift, col_shift)

    light[...] = canvas[height : 2 * height, width : 2 * width] + 1.0


def run_light(height, width, slots, info, probe):
    pattern = probe.shape[-1]
    return pl.pallas_call(
        functools.partial(light_kernel, height, width, slots),
        out_shape=jax.ShapeDtypeStruct((height, width), jnp.float32),
        in_specs=[pl.BlockSpec(memory_space=pltpu.SMEM), pl.BlockSpec(memory_space=pltpu.VMEM)],
        out_specs=pl.BlockSpec(memory_space=pltpu.VMEM),
        scratch_shapes=[
            pltpu.VMEM((2 * height + pattern, 2 * width + pattern), jnp.float32),
            pltpu.VMEM((pattern + sublanes, pattern + lanes), jnp.float32),
        ],
        compiler_params=pltpu.CompilerParams(vmem_limit_bytes=24 * 1024 * 1024),
        cost_estimate=pl.CostEstimate(flops=10_000_000, bytes_accessed=12_000_000, transcendentals=0),
    )(info, probe)


def final_kernel(tile, grad, left, above, light, out):
    pattern = left.shape[-1]
    grad[0, 0, :, :pattern] = grad[0, 0, :, :pattern] + left[0, 0]
    grad[0, 0, :pattern, :] = grad[0, 0, :pattern, :] + above[0, 0]
    out[0, 0] = tile[0, 0] - grad[0, 0] / light[...]


def run_final(tile, grad, left, above, light):
    layers, parts, height, width = tile.shape
    spec = lambda array: pl.BlockSpec((1, 1) + array.shape[2:], lambda i, j: (i, j, 0, 0))
    return pl.pallas_call(
        final_kernel,
        grid=(layers, parts),
        out_shape=jax.ShapeDtypeStruct(tile.shape, jnp.float32),
        in_specs=[spec(tile), spec(grad), spec(left), spec(above), pl.BlockSpec(light.shape, lambda i, j: (0, 0))],
        out_specs=spec(tile),
        compiler_params=pltpu.CompilerParams(vmem_limit_bytes=24 * 1024 * 1024),
        cost_estimate=pl.CostEstimate(flops=4_000_000, bytes_accessed=14_000_000, transcendentals=0),
    )(tile, grad, left, above, light)


def on_device(object_slab, probe_mode_stack, offsets, measured, counts):
    tile_height = object_slab.shape[2]
    tile_width = object_slab.shape[3]
    pattern = probe_mode_stack.shape[-1]
    slots = offsets.shape[0]
    table_f = dft_matrix(pattern, -1.0)
    table_b = dft_matrix(pattern, 1.0)
    fresnel = propagator(pattern)
    right_rim = from_behind(object_slab[:, :, :, :pattern], "scan", -1)
    lower_rim = from_behind(object_slab[:, :, :pattern, :], "obj", -1)
    corner_rim = from_behind(right_rim[:, :, :pattern, :], "obj", -1)
    base = jnp.stack([lax.axis_index("obj") * tile_height, lax.axis_index("scan") * tile_width])
    base = base.astype(jnp.int32)
    corners = offsets - base
    own_info = jnp.concatenate([offsets.reshape(-1), counts])
    left_info = from_behind(own_info, "scan", 1)
    row_info = jnp.concatenate([own_info, left_info])
    info = jnp.concatenate([row_info, from_behind(row_info, "obj", 1)])
    shifts = jnp.tile(jnp.concatenate([jnp.tile(base, slots), jnp.zeros((1,), jnp.int32)]), 4)
    light = run_light(tile_height, tile_width, slots, info - shifts, probe_mode_stack)
    grad_tile, grad_right, grad_lower, grad_corner, grad_probe = run_slots(
        corners, counts, object_slab, right_rim, lower_rim, corner_rim, probe_mode_stack,
        measured, table_f, table_b, fresnel,
    )
    corner_half = from_behind(grad_corner, "scan", 1)
    from_left = from_behind(grad_right, "scan", 1)
    grad_lower = grad_lower.at[:, :, :, :pattern].add(corner_half)
    from_above = from_behind(grad_lower, "obj", 1)
    new_object = run_final(object_slab, grad_tile, from_left, from_above, light)
    summed = lax.psum(grad_probe, ("obj", "scan"))
    grad_scale = jnp.sqrt(jnp.mean(summed * summed) + 1e-06)
    new_probe = probe_mode_stack - probe_step * summed / grad_scale
    return (new_object, new_probe)


def solution(mesh):
    in_specs = (
        P(None, None, "obj", "scan"),
        P(),
        P(("obj", "scan"), None),
        P(("obj", "scan"), None, None),
        P(("obj", "scan")),
    )
    out_specs = (P(None, None, "obj", "scan"), P())
    return jax.shard_map(
        on_device, mesh=mesh, in_specs=in_specs, out_specs=out_specs, check_vma=False
    )
```

```python
import functools
import math

import jax
import jax.numpy as jnp
import numpy as np
from jax import lax
from jax.experimental import pallas as pl
from jax.experimental.pallas import tpu as pltpu
from jax.sharding import PartitionSpec as P

chirp_scale = 24.0
probe_step = 0.15
lanes = 128
sublanes = 8
vmem_bytes = 56 * 1024 * 1024


def from_behind(array, axis, by):
    count = lax.axis_size(axis)
    pairs = [(i, i + by) for i in range(count) if 0 <= i + by < count]
    return lax.ppermute(array, axis, pairs)


def dft_matrix(pattern, sign_factor):
    indices = np.arange(pattern)
    angles = (indices[:, None] * indices[None, :] % pattern) * (2.0 * math.pi / pattern)
    real_part = np.cos(angles) / math.sqrt(pattern)
    imag_part = sign_factor * np.sin(angles) / math.sqrt(pattern)
    upper = np.concatenate([real_part, -imag_part], axis=1)
    lower = np.concatenate([imag_part, real_part], axis=1)
    return jnp.asarray(np.concatenate([upper, lower], axis=0).astype(np.float32), jnp.bfloat16)


def propagator(pattern):
    indices = np.arange(pattern)
    freqs = ((indices + pattern // 2) % pattern - pattern // 2) / pattern
    phases = -math.pi * chirp_scale * (freqs[:, None] ** 2 + freqs[None, :] ** 2)
    return jnp.asarray(np.stack([np.cos(phases), np.sin(phases)], axis=0).astype(np.float32))


def aligned(row, col):
    row_base = pl.multiple_of(row // sublanes * sublanes, sublanes)
    col_base = pl.multiple_of(col // lanes * lanes, lanes)
    return row_base, col_base, row - row_base, col - col_base


def pad(array):
    array = jnp.concatenate([array, jnp.zeros((array.shape[0], lanes), jnp.float32)], axis=1)
    return jnp.concatenate([array, jnp.zeros((sublanes, array.shape[1]), jnp.float32)], axis=0)


def roll_down(array, rows, cols):
    return pltpu.roll(pltpu.roll(array, cols, 1), rows, 0)


def transform(real_part, imag_part, left, right):
    pattern = real_part.shape[0]
    stacked = jnp.concatenate([real_part.astype(jnp.bfloat16), imag_part.astype(jnp.bfloat16)], axis=0)
    half = jnp.dot(left, stacked, preferred_element_type=jnp.float32).astype(jnp.bfloat16)
    half = jnp.concatenate([half[:pattern], half[pattern:]], axis=1)
    full = jnp.dot(half, right, preferred_element_type=jnp.float32)
    return full[:, :pattern], full[:, pattern:]


def slots_kernel(
    corners, used, tile, right, lower, corner, probe, measured, table_f, table_b, fresnel,
    grad_tile, grad_right, grad_lower, grad_corner, grad_probe,
    ext, grad, window, waves, far, intensity, term, sems_in, sems_out,
):
    modes, _, pattern, _ = probe.shape
    layers = tile.shape[0]
    height, width = tile.shape[2], tile.shape[3]
    wide = pattern + lanes
    tall = pattern + sublanes

    def spots(buffer):
        return (
            buffer.at[:, :, pl.ds(0, height), pl.ds(0, width)],
            buffer.at[:, :, pl.ds(0, height), pl.ds(width, pattern)],
            buffer.at[:, :, pl.ds(height, pattern), pl.ds(0, width)],
            buffer.at[:, :, pl.ds(height, pattern), pl.ds(width, pattern)],
        )

    loads = [
        pltpu.make_async_copy(source, spot, sems_in.at[k])
        for k, (source, spot) in enumerate(zip((tile, right, lower, corner), spots(ext)))
    ]
    for load in loads:
        load.start()
    grad[...] = jnp.zeros_like(grad)
    grad_probe[...] = jnp.zeros_like(grad_probe)
    for load in loads:
        load.wait()

    @pl.loop(0, used[0])
    def _(slot):
        row = corners[slot, 0]
        col = corners[slot, 1]
        row_base, col_base, row_shift, col_shift = aligned(row, col)
        row_back = jnp.where(row_shift == 0, 0, tall - row_shift)
        col_back = jnp.where(col_shift == 0, 0, wide - col_shift)
        for layer in range(layers):
            for part in range(2):
                block = ext[layer, part, pl.ds(row_base, tall), pl.ds(col_base, wide)]
                window[layer, part] = roll_down(block, row_back, col_back)[:pattern, :pattern]
        intensity[...] = jnp.zeros_like(intensity)
        term[...] = jnp.zeros_like(term)

        @pl.loop(0, modes, unroll=2)
        def _(mode):
            wr, wi = probe[mode, 0], probe[mode, 1]
            for layer in range(layers):
                o_r, o_i = window[layer, 0], window[layer, 1]
                fr, fi = transform(o_r * wr - o_i * wi, o_r * wi + o_i * wr, table_f[...], table_b[...])
                if layer < layers - 1:
                    hr, hi = fresnel[0], fresnel[1]
                    wr, wi = transform(hr * fr - hi * fi, hr * fi + hi * fr, table_b[...], table_f[...])
                    waves[layer, mode, 0] = wr
                    waves[layer, mode, 1] = wi
            far[mode, 0] = fr
            far[mode, 1] = fi
            intensity[...] += fr * fr + fi * fi

        intensity[...] = intensity[...] - measured[slot]

        @pl.loop(0, modes, unroll=2)
        def _(mode):
            gain = intensity[...]
            gr, gi = transform(gain * far[mode, 0], gain * far[mode, 1], table_b[...], table_f[...])
            for layer in reversed(range(layers)):
                if layer < layers - 1:
                    sr, si = transform(gr, gi, table_f[...], table_b[...])
                    hr, hi = fresnel[0], fresnel[1]
                    gr, gi = transform(hr * sr + hi * si, hr * si - hi * sr, table_b[...], table_f[...])
                if layer == 0:
                    wr, wi = probe[mode, 0], probe[mode, 1]
                else:
                    wr, wi = waves[layer - 1, mode, 0], waves[layer - 1, mode, 1]
                term[layer, 0] += wr * gr + wi * gi
                term[layer, 1] += wr * gi - wi * gr
                o_r, o_i = window[layer, 0], window[layer, 1]
                gr, gi = o_r * gr + o_i * gi, o_r * gi - o_i * gr
            grad_probe[mode, 0] += gr
            grad_probe[mode, 1] += gi

        for layer in range(layers):
            for part in range(2):
                at = (layer, part, pl.ds(row_base, tall), pl.ds(col_base, wide))
                grad[at] = grad[at] + roll_down(pad(term[layer, part]), row_shift, col_shift)

    saves = [
        pltpu.make_async_copy(spot, target, sems_out.at[k])
        for k, (spot, target) in enumerate(
            zip(spots(grad), (grad_tile, grad_right, grad_lower, grad_corner))
        )
    ]
    for save in saves:
        save.start()
    for save in saves:
        save.wait()


def run_slots(corners, used, tile, right, lower, corner, probe, measured, table_f, table_b, fresnel):
    layers, _, height, width = tile.shape
    modes, _, pattern, _ = probe.shape
    smem = pl.BlockSpec(memory_space=pltpu.SMEM)
    vmem = pl.BlockSpec(memory_space=pltpu.VMEM)
    anyw = pl.BlockSpec(memory_space=pl.ANY)
    f32 = jnp.float32
    ext_shape = (layers, 2, height + pattern, width + pattern)
    return pl.pallas_call(
        slots_kernel,
        out_shape=(
            jax.ShapeDtypeStruct(tile.shape, f32),
            jax.ShapeDtypeStruct(right.shape, f32),
            jax.ShapeDtypeStruct(lower.shape, f32),
            jax.ShapeDtypeStruct(corner.shape, f32),
            jax.ShapeDtypeStruct(probe.shape, f32),
        ),
        in_specs=[smem, smem, anyw, anyw, anyw, anyw, vmem, vmem, vmem, vmem, vmem],
        out_specs=(anyw, anyw, anyw, anyw, vmem),
        scratch_shapes=[
            pltpu.VMEM(ext_shape, f32),
            pltpu.VMEM(ext_shape, f32),
            pltpu.VMEM((layers, 2, pattern, pattern), f32),
            pltpu.VMEM((layers - 1, modes, 2, pattern, pattern), f32),
            pltpu.VMEM((modes, 2, pattern, pattern), f32),
            pltpu.VMEM((pattern, pattern), f32),
            pltpu.VMEM((layers, 2, pattern, pattern), f32),
            pltpu.SemaphoreType.DMA((4,)),
            pltpu.SemaphoreType.DMA((4,)),
        ],
        compiler_params=pltpu.CompilerParams(vmem_limit_bytes=vmem_bytes),
        cost_estimate=pl.CostEstimate(flops=29_000_000_000, bytes_accessed=30_000_000, transcendentals=0),
    )(corners, used, tile, right, lower, corner, probe, measured, table_f, table_b, fresnel)


def light_kernel(height, width, slots, info, probe, light, canvas, power):
    modes, _, pattern, _ = probe.shape
    total = jnp.zeros((pattern, pattern), jnp.float32)
    for mode in range(modes):
        total = total + (probe[mode, 0] * probe[mode, 0] + probe[mode, 1] * probe[mode, 1])
    power[...] = pad(total)
    canvas[...] = jnp.zeros_like(canvas)
    for block in range(4):
        base = block * (2 * slots + 1)

        @pl.loop(0, info[base + 2 * slots])
        def _(slot):
            row = info[base + 2 * slot] + height
            col = info[base + 2 * slot + 1] + width
            row_base, col_base, row_shift, col_shift = aligned(row, col)
            at = (pl.ds(row_base, pattern + sublanes), pl.ds(col_base, pattern + lanes))
            canvas[at] = canvas[at] + roll_down(power[...], row_shift, col_shift)

    light[...] = canvas[height : 2 * height, width : 2 * width] + 1.0


def run_light(height, width, slots, info, probe):
    pattern = probe.shape[-1]
    return pl.pallas_call(
        functools.partial(light_kernel, height, width, slots),
        out_shape=jax.ShapeDtypeStruct((height, width), jnp.float32),
        in_specs=[pl.BlockSpec(memory_space=pltpu.SMEM), pl.BlockSpec(memory_space=pltpu.VMEM)],
        out_specs=pl.BlockSpec(memory_space=pltpu.VMEM),
        scratch_shapes=[
            pltpu.VMEM((2 * height + pattern, 2 * width + pattern), jnp.float32),
            pltpu.VMEM((pattern + sublanes, pattern + lanes), jnp.float32),
        ],
        compiler_params=pltpu.CompilerParams(vmem_limit_bytes=24 * 1024 * 1024),
        cost_estimate=pl.CostEstimate(flops=10_000_000, bytes_accessed=12_000_000, transcendentals=0),
    )(info, probe)


def final_kernel(tile, grad, left, above, corner, light, out):
    pattern = left.shape[-1]
    grad[0, 0, :, :pattern] = grad[0, 0, :, :pattern] + left[0, 0]
    grad[0, 0, :pattern, :] = grad[0, 0, :pattern, :] + above[0, 0]
    grad[0, 0, :pattern, :pattern] = grad[0, 0, :pattern, :pattern] + corner[0, 0]
    out[0, 0] = tile[0, 0] - grad[0, 0] / light[...]


def run_final(tile, grad, left, above, corner, light):
    layers, parts, height, width = tile.shape
    spec = lambda array: pl.BlockSpec((1, 1) + array.shape[2:], lambda i, j: (i, j, 0, 0))
    return pl.pallas_call(
        final_kernel,
        grid=(layers, parts),
        out_shape=jax.ShapeDtypeStruct(tile.shape, jnp.float32),
        in_specs=[
            spec(tile), spec(grad), spec(left), spec(above), spec(corner),
            pl.BlockSpec(light.shape, lambda i, j: (0, 0)),
        ],
        out_specs=spec(tile),
        compiler_params=pltpu.CompilerParams(vmem_limit_bytes=24 * 1024 * 1024),
        cost_estimate=pl.CostEstimate(flops=4_000_000, bytes_accessed=14_000_000, transcendentals=0),
    )(tile, grad, left, above, corner, light)


def on_device(object_slab, probe_mode_stack, offsets, measured, counts):
    tile_height = object_slab.shape[2]
    tile_width = object_slab.shape[3]
    pattern = probe_mode_stack.shape[-1]
    slots = offsets.shape[0]
    table_f = dft_matrix(pattern, -1.0)
    table_b = dft_matrix(pattern, 1.0)
    fresnel = propagator(pattern)
    right_rim = from_behind(object_slab[:, :, :, :pattern], "scan", -1)
    lower_rim = from_behind(object_slab[:, :, :pattern, :], "obj", -1)
    corner_rim = from_behind(right_rim[:, :, :pattern, :], "obj", -1)
    base = jnp.stack([lax.axis_index("obj") * tile_height, lax.axis_index("scan") * tile_width])
    base = base.astype(jnp.int32)
    corners = offsets - base
    own_info = jnp.concatenate([offsets.reshape(-1), counts])
    left_info = from_behind(own_info, "scan", 1)
    row_info = jnp.concatenate([own_info, left_info])
    info = jnp.concatenate([row_info, from_behind(row_info, "obj", 1)])
    right_rim, lower_rim, corner_rim, corners, info = lax.optimization_barrier(
        (right_rim, lower_rim, corner_rim, corners, info)
    )
    shifts = jnp.tile(jnp.concatenate([jnp.tile(base, slots), jnp.zeros((1,), jnp.int32)]), 4)
    light = run_light(tile_height, tile_width, slots, info - shifts, probe_mode_stack)
    grad_tile, grad_right, grad_lower, grad_corner, grad_probe = run_slots(
        corners, counts, object_slab, right_rim, lower_rim, corner_rim, probe_mode_stack,
        measured, table_f, table_b, fresnel,
    )
    summed = lax.psum(grad_probe, ("obj", "scan"))
    corner_half = from_behind(grad_corner, "obj", 1)
    from_above = from_behind(grad_lower, "obj", 1)
    from_left = from_behind(grad_right, "scan", 1)
    from_corner = from_behind(corner_half, "scan", 1)
    new_object = run_final(object_slab, grad_tile, from_left, from_above, from_corner, light)
    summed, new_object = lax.optimization_barrier((summed, new_object))
    grad_scale = jnp.sqrt(jnp.mean(summed * summed) + 1e-06)
    new_probe = probe_mode_stack - probe_step * summed / grad_scale
    return (new_object, new_probe)


def solution(mesh):
    in_specs = (
        P(None, None, "obj", "scan"),
        P(),
        P(("obj", "scan"), None),
        P(("obj", "scan"), None, None),
        P(("obj", "scan")),
    )
    out_specs = (P(None, None, "obj", "scan"), P())
    return jax.shard_map(
        on_device, mesh=mesh, in_specs=in_specs, out_specs=out_specs, check_vma=False
    )
```

```python
import functools
import math

import jax
import jax.numpy as jnp
import numpy as np
from jax import lax
from jax.experimental import pallas as pl
from jax.experimental.pallas import tpu as pltpu
from jax.sharding import PartitionSpec as P

chirp_scale = 24.0
probe_step = 0.15
lanes = 128
sublanes = 8
vmem_bytes = 56 * 1024 * 1024


def from_behind(array, axis, by):
    count = lax.axis_size(axis)
    pairs = [(i, i + by) for i in range(count) if 0 <= i + by < count]
    return lax.ppermute(array, axis, pairs)


def dft_matrix(pattern, sign_factor):
    indices = np.arange(pattern)
    angles = (indices[:, None] * indices[None, :] % pattern) * (2.0 * math.pi / pattern)
    real_part = np.cos(angles) / math.sqrt(pattern)
    imag_part = sign_factor * np.sin(angles) / math.sqrt(pattern)
    upper = np.concatenate([real_part, -imag_part], axis=1)
    lower = np.concatenate([imag_part, real_part], axis=1)
    return jnp.asarray(np.concatenate([upper, lower], axis=0).astype(np.float32), jnp.bfloat16)


def propagator(pattern):
    indices = np.arange(pattern)
    freqs = ((indices + pattern // 2) % pattern - pattern // 2) / pattern
    phases = -math.pi * chirp_scale * (freqs[:, None] ** 2 + freqs[None, :] ** 2)
    return jnp.asarray(np.stack([np.cos(phases), np.sin(phases)], axis=0).astype(np.float32))


def aligned(row, col):
    row_base = pl.multiple_of(row // sublanes * sublanes, sublanes)
    col_base = pl.multiple_of(col // lanes * lanes, lanes)
    return row_base, col_base, row - row_base, col - col_base


def pad(array):
    array = jnp.concatenate([array, jnp.zeros((array.shape[0], lanes), jnp.float32)], axis=1)
    return jnp.concatenate([array, jnp.zeros((sublanes, array.shape[1]), jnp.float32)], axis=0)


def roll_down(array, rows, cols):
    return pltpu.roll(pltpu.roll(array, cols, 1), rows, 0)


def transform(real_part, imag_part, left, right):
    pattern = real_part.shape[0]
    stacked = jnp.concatenate([real_part.astype(jnp.bfloat16), imag_part.astype(jnp.bfloat16)], axis=0)
    half = jnp.dot(left, stacked, preferred_element_type=jnp.float32).astype(jnp.bfloat16)
    half = jnp.concatenate([half[:pattern], half[pattern:]], axis=1)
    full = jnp.dot(half, right, preferred_element_type=jnp.float32)
    return full[:, :pattern], full[:, pattern:]


def slots_kernel(
    corners, used, tile, right, lower, corner, probe, measured, table_f, table_b, fresnel,
    grad_tile, grad_right, grad_lower, grad_corner, grad_probe,
    ext, grad, window, waves, far, intensity, term, sems_in, sems_out,
):
    modes, _, pattern, _ = probe.shape
    layers = tile.shape[0]
    height, width = tile.shape[2], tile.shape[3]
    wide = pattern + lanes
    tall = pattern + sublanes

    def spots(buffer):
        return (
            buffer.at[:, :, pl.ds(0, height), pl.ds(0, width)],
            buffer.at[:, :, pl.ds(0, height), pl.ds(width, pattern)],
            buffer.at[:, :, pl.ds(height, pattern), pl.ds(0, width)],
            buffer.at[:, :, pl.ds(height, pattern), pl.ds(width, pattern)],
        )

    loads = [
        pltpu.make_async_copy(source, spot, sems_in.at[k])
        for k, (source, spot) in enumerate(zip((tile, right, lower, corner), spots(ext)))
    ]
    for load in loads:
        load.start()
    grad[...] = jnp.zeros_like(grad)
    grad_probe[...] = jnp.zeros_like(grad_probe)
    for load in loads:
        load.wait()

    @pl.loop(0, used[0])
    def _(slot):
        row = corners[slot, 0]
        col = corners[slot, 1]
        row_base, col_base, row_shift, col_shift = aligned(row, col)
        row_back = jnp.where(row_shift == 0, 0, tall - row_shift)
        col_back = jnp.where(col_shift == 0, 0, wide - col_shift)
        for layer in range(layers):
            for part in range(2):
                block = ext[layer, part, pl.ds(row_base, tall), pl.ds(col_base, wide)]
                window[layer, part] = roll_down(block, row_back, col_back)[:pattern, :pattern]
        intensity[...] = jnp.zeros_like(intensity)
        term[...] = jnp.zeros_like(term)

        @pl.loop(0, modes, unroll=2)
        def _(mode):
            wr, wi = probe[mode, 0], probe[mode, 1]
            for layer in range(layers):
                o_r, o_i = window[layer, 0], window[layer, 1]
                fr, fi = transform(o_r * wr - o_i * wi, o_r * wi + o_i * wr, table_f[...], table_b[...])
                if layer < layers - 1:
                    hr, hi = fresnel[0], fresnel[1]
                    wr, wi = transform(hr * fr - hi * fi, hr * fi + hi * fr, table_b[...], table_f[...])
                    waves[layer, mode, 0] = wr
                    waves[layer, mode, 1] = wi
            far[mode, 0] = fr
            far[mode, 1] = fi
            intensity[...] += fr * fr + fi * fi

        intensity[...] = intensity[...] - measured[slot]

        @pl.loop(0, modes, unroll=2)
        def _(mode):
            gain = intensity[...]
            gr, gi = transform(gain * far[mode, 0], gain * far[mode, 1], table_b[...], table_f[...])
            for layer in reversed(range(layers)):
                if layer < layers - 1:
                    sr, si = transform(gr, gi, table_f[...], table_b[...])
                    hr, hi = fresnel[0], fresnel[1]
                    gr, gi = transform(hr * sr + hi * si, hr * si - hi * sr, table_b[...], table_f[...])
                if layer == 0:
                    wr, wi = probe[mode, 0], probe[mode, 1]
                else:
                    wr, wi = waves[layer - 1, mode, 0], waves[layer - 1, mode, 1]
                term[layer, 0] += wr * gr + wi * gi
                term[layer, 1] += wr * gi - wi * gr
                o_r, o_i = window[layer, 0], window[layer, 1]
                gr, gi = o_r * gr + o_i * gi, o_r * gi - o_i * gr
            grad_probe[mode, 0] += gr
            grad_probe[mode, 1] += gi

        for layer in range(layers):
            for part in range(2):
                at = (layer, part, pl.ds(row_base, tall), pl.ds(col_base, wide))
                grad[at] = grad[at] + roll_down(pad(term[layer, part]), row_shift, col_shift)

    saves = [
        pltpu.make_async_copy(spot, target, sems_out.at[k])
        for k, (spot, target) in enumerate(
            zip(spots(grad), (grad_tile, grad_right, grad_lower, grad_corner))
        )
    ]
    for save in saves:
        save.start()
    for save in saves:
        save.wait()


def run_slots(corners, used, tile, right, lower, corner, probe, measured, table_f, table_b, fresnel):
    layers, _, height, width = tile.shape
    modes, _, pattern, _ = probe.shape
    smem = pl.BlockSpec(memory_space=pltpu.SMEM)
    vmem = pl.BlockSpec(memory_space=pltpu.VMEM)
    anyw = pl.BlockSpec(memory_space=pl.ANY)
    f32 = jnp.float32
    ext_shape = (layers, 2, height + pattern, width + pattern)
    return pl.pallas_call(
        slots_kernel,
        out_shape=(
            jax.ShapeDtypeStruct(tile.shape, f32),
            jax.ShapeDtypeStruct(right.shape, f32),
            jax.ShapeDtypeStruct(lower.shape, f32),
            jax.ShapeDtypeStruct(corner.shape, f32),
            jax.ShapeDtypeStruct(probe.shape, f32),
        ),
        in_specs=[smem, smem, anyw, anyw, anyw, anyw, vmem, vmem, vmem, vmem, vmem],
        out_specs=(anyw, anyw, anyw, anyw, vmem),
        scratch_shapes=[
            pltpu.VMEM(ext_shape, f32),
            pltpu.VMEM(ext_shape, f32),
            pltpu.VMEM((layers, 2, pattern, pattern), f32),
            pltpu.VMEM((layers - 1, modes, 2, pattern, pattern), f32),
            pltpu.VMEM((modes, 2, pattern, pattern), f32),
            pltpu.VMEM((pattern, pattern), f32),
            pltpu.VMEM((layers, 2, pattern, pattern), f32),
            pltpu.SemaphoreType.DMA((4,)),
            pltpu.SemaphoreType.DMA((4,)),
        ],
        compiler_params=pltpu.CompilerParams(vmem_limit_bytes=vmem_bytes),
        cost_estimate=pl.CostEstimate(flops=29_000_000_000, bytes_accessed=30_000_000, transcendentals=0),
    )(corners, used, tile, right, lower, corner, probe, measured, table_f, table_b, fresnel)


def light_kernel(height, width, slots, info, probe, light, canvas, power):
    modes, _, pattern, _ = probe.shape
    total = jnp.zeros((pattern, pattern), jnp.float32)
    for mode in range(modes):
        total = total + (probe[mode, 0] * probe[mode, 0] + probe[mode, 1] * probe[mode, 1])
    power[...] = pad(total)
    canvas[...] = jnp.zeros_like(canvas)
    for block in range(4):
        base = block * (2 * slots + 1)

        @pl.loop(0, info[base + 2 * slots])
        def _(slot):
            row = info[base + 2 * slot] + height
            col = info[base + 2 * slot + 1] + width
            row_base, col_base, row_shift, col_shift = aligned(row, col)
            at = (pl.ds(row_base, pattern + sublanes), pl.ds(col_base, pattern + lanes))
            canvas[at] = canvas[at] + roll_down(power[...], row_shift, col_shift)

    light[...] = canvas[height : 2 * height, width : 2 * width] + 1.0


def run_light(height, width, slots, info, probe):
    pattern = probe.shape[-1]
    return pl.pallas_call(
        functools.partial(light_kernel, height, width, slots),
        out_shape=jax.ShapeDtypeStruct((height, width), jnp.float32),
        in_specs=[pl.BlockSpec(memory_space=pltpu.SMEM), pl.BlockSpec(memory_space=pltpu.VMEM)],
        out_specs=pl.BlockSpec(memory_space=pltpu.VMEM),
        scratch_shapes=[
            pltpu.VMEM((2 * height + pattern, 2 * width + pattern), jnp.float32),
            pltpu.VMEM((pattern + sublanes, pattern + lanes), jnp.float32),
        ],
        compiler_params=pltpu.CompilerParams(vmem_limit_bytes=24 * 1024 * 1024),
        cost_estimate=pl.CostEstimate(flops=10_000_000, bytes_accessed=12_000_000, transcendentals=0),
    )(info, probe)


def final_kernel(tile, grad, left, above, light, out):
    pattern = left.shape[-1]
    grad[0, 0, :, :pattern] = grad[0, 0, :, :pattern] + left[0, 0]
    grad[0, 0, :pattern, :] = grad[0, 0, :pattern, :] + above[0, 0]
    out[0, 0] = tile[0, 0] - grad[0, 0] / light[...]


def run_final(tile, grad, left, above, light):
    layers, parts, height, width = tile.shape
    spec = lambda array: pl.BlockSpec((1, 1) + array.shape[2:], lambda i, j: (i, j, 0, 0))
    return pl.pallas_call(
        final_kernel,
        grid=(layers, parts),
        out_shape=jax.ShapeDtypeStruct(tile.shape, jnp.float32),
        in_specs=[
            spec(tile), spec(grad), spec(left), spec(above),
            pl.BlockSpec(light.shape, lambda i, j: (0, 0)),
        ],
        out_specs=spec(tile),
        compiler_params=pltpu.CompilerParams(vmem_limit_bytes=24 * 1024 * 1024),
        cost_estimate=pl.CostEstimate(flops=4_000_000, bytes_accessed=14_000_000, transcendentals=0),
    )(tile, grad, left, above, light)


def on_device(object_slab, probe_mode_stack, offsets, measured, counts):
    tile_height = object_slab.shape[2]
    tile_width = object_slab.shape[3]
    pattern = probe_mode_stack.shape[-1]
    slots = offsets.shape[0]
    table_f = dft_matrix(pattern, -1.0)
    table_b = dft_matrix(pattern, 1.0)
    fresnel = propagator(pattern)
    right_rim = from_behind(object_slab[:, :, :, :pattern], "scan", -1)
    lower_rim = from_behind(object_slab[:, :, :pattern, :], "obj", -1)
    corner_rim = from_behind(right_rim[:, :, :pattern, :], "obj", -1)
    base = jnp.stack([lax.axis_index("obj") * tile_height, lax.axis_index("scan") * tile_width])
    base = base.astype(jnp.int32)
    corners = offsets - base
    own_info = jnp.concatenate([offsets.reshape(-1), counts])
    left_info = from_behind(own_info, "scan", 1)
    row_info = jnp.concatenate([own_info, left_info])
    info = jnp.concatenate([row_info, from_behind(row_info, "obj", 1)])
    right_rim, lower_rim, corner_rim, corners, info = lax.optimization_barrier(
        (right_rim, lower_rim, corner_rim, corners, info)
    )
    shifts = jnp.tile(jnp.concatenate([jnp.tile(base, slots), jnp.zeros((1,), jnp.int32)]), 4)
    light = run_light(tile_height, tile_width, slots, info - shifts, probe_mode_stack)
    grad_tile, grad_right, grad_lower, grad_corner, grad_probe = run_slots(
        corners, counts, object_slab, right_rim, lower_rim, corner_rim, probe_mode_stack,
        measured, table_f, table_b, fresnel,
    )
    summed = lax.psum(grad_probe, ("obj", "scan"))
    corner_half = from_behind(grad_corner, "obj", 1)
    from_above = from_behind(grad_lower, "obj", 1)
    grad_right = grad_right.at[:, :, :pattern, :].add(corner_half)
    from_left = from_behind(grad_right, "scan", 1)
    new_object = run_final(object_slab, grad_tile, from_left, from_above, light)
    summed, new_object = lax.optimization_barrier((summed, new_object))
    grad_scale = jnp.sqrt(jnp.mean(summed * summed) + 1e-06)
    new_probe = probe_mode_stack - probe_step * summed / grad_scale
    return (new_object, new_probe)


def solution(mesh):
    in_specs = (
        P(None, None, "obj", "scan"),
        P(),
        P(("obj", "scan"), None),
        P(("obj", "scan"), None, None),
        P(("obj", "scan")),
    )
    out_specs = (P(None, None, "obj", "scan"), P())
    return jax.shard_map(
        on_device, mesh=mesh, in_specs=in_specs, out_specs=out_specs, check_vma=False
    )
```
